1024 devices in a mesh: node: 8 (over x), local: 128 (over z, y, core).
Axes of the slice: x: 8, y: 8, z: 8, core: 2. Of those that a mesh axis runs over, the one named last changes fastest.
Arguments:
- tokens: bfloat16 [1024, 3584], P('node', 'local'), may hold values from -6 to 6
- out_grad: bfloat16 [1024, 3584], P('node', 'local'), may hold values from -6 to 6
- expert_ids: int32 [1024, 8], P('node'), may hold values from 0 to 127, all different within a row; in each aligned block of 128 rows (0 to 127, 128 to 255, ...) at most 16 rows name the same one
- gate_weights: float32 [1024, 8], P('node'), may hold values from 0.02 to 0.5
- gate_weight: bfloat16 [1024, 3584, 128], P(('node', 'local')), may hold values from -0.09375 to 0.09375
- up_weight: bfloat16 [1024, 3584, 128], P(('node', 'local')), may hold values from -0.09375 to 0.09375
- down_weight: bfloat16 [1024, 128, 3584], P(('node', 'local')), may hold values from -0.1875 to 0.1875
Outputs:
- token_grad: bfloat16 [1024, 3584], P('node', 'local')
- gate_grad: float32 [1024, 8], P('node')
The draws below stay inside these ranges and needn't reach their ends.
Inputs may be any that keep to these rules, and one draw needn't show every extreme that they name: `expert_ids`: each row names 8 different experts. Among the 128 tokens of one node group (aligned blocks of 128 rows) no expert is named by more than 16 rows, a bound that some block reaches.
All inputs are finite; a program needn't handle non-finite values.
Results may differ from the reference program's by a relative error of at most 0.014.
Values may be sent and summed in bfloat16 or wider, within the bound.
A program may use at most 32 MiB of HBM per device.

```python
import math
import jax
import jax.numpy as jnp
import numpy as np
from jax import lax

D = 3584
FF = 1024
TOPK = 8
SPLIT = 8
TOK_NODE = 128
EXPERTS = 128
HID = 128
CAP = 16
TOKENS = 1024
N_NODE = 8


def block_levels(rng, shape, pieces, smallest, largest):
    def one(axis_at, shards_of):
        heights = jax.random.uniform(jax.random.fold_in(jax.random.fold_in(rng, 6), axis_at), (shards_of,), jnp.float32, smallest / len(pieces), largest / len(pieces))
        return jnp.repeat(jnp.exp(heights), shape[axis_at] // shards_of).reshape((-1,) + (1,) * (len(shape) - axis_at - 1))

    factor_of = one(*pieces[0])
    for cut in pieces[1:]:
        factor_of = factor_of * one(*cut)
    return factor_of


def shared_out(stream_key, own, number, rows, count, top, most, skew):
    ranking = jax.random.permutation(stream_key, count)
    crowded, common = load_shares(count, rows * top, most, skew, True), load_shares(count, rows * top, most, skew, False)
    places = jnp.arange(count)

    def named(lengths, rotation):
        used = int((lengths > 0).sum())
        fixed = max(1, used // 4)
        shifted = fixed + (places - fixed + rotation * (used - fixed)) % max(1, count - fixed)
        return jnp.zeros((count,), jnp.int32).at[ranking[jnp.where(places < fixed, places, shifted)]].set(jnp.asarray(lengths, jnp.int32))

    lengths = jnp.where(number % 4 == 0, named(crowded, number // 4), named(common, number - number // 4 - 1))
    mixed = jax.random.permutation(jax.random.fold_in(own, 3), count)
    giver, receiver = mixed[0:count // 2 * 2:2], mixed[1:count // 2 * 2:2]
    room = jnp.minimum(lengths[giver] - 1, most - lengths[receiver]) // 2
    room = jnp.where((giver == ranking[0]) | (receiver == ranking[0]) | (lengths[receiver] == 0), 0, jnp.maximum(room, 0))
    shifted = jax.random.randint(jax.random.fold_in(own, 4), (count // 2,), 0, 1 << 20) % (room + 1)
    lengths = lengths.at[giver].add(-shifted).at[receiver].add(shifted)
    items = jnp.searchsorted(jnp.cumsum(lengths), jnp.arange(rows * top), side="right").astype(jnp.int32)
    table = items.reshape(top, rows).T
    table = table[jax.random.permutation(jax.random.fold_in(own, 1), rows)]
    rotation = jax.random.randint(jax.random.fold_in(own, 2), (rows, 1), 0, top)
    return jnp.take_along_axis(table, (jnp.arange(top)[None, :] + rotation) % top, axis=1)


def load_shares(amount, total, reach, lean, full):
    weights = [(1 << 20) // math.isqrt(rank ** lean) + 1 for rank in range(1, amount + 1)]
    largest = reach if full else min(reach, max(-(-total // amount), total * weights[0] // sum(weights)))
    least = 1 if total - largest >= amount - 1 else 0
    counts, spare = [largest] + [least] * (amount - 1), total - largest - least * (amount - 1)
    while spare > 0:
        movable = [i for i in range(1, amount) if counts[i] < largest] or [i for i in range(1, amount) if counts[i] < reach]
        pool, budget = sum([weights[i] for i in movable]), spare
        for i in movable:
            more = min(reach - counts[i], max(1, budget * weights[i] // pool), spare)
            counts[i] = counts[i] + more
            spare = spare - more
    return np.array(counts)


def scatter_about(rng, extent, spread, most, shards=(), kind=jnp.bfloat16):
    array = jax.random.normal(rng, extent, jnp.float32) * spread
    if len(shards) > 0:
        array = block_levels(rng, extent, shards, -0.22, 0.18) * array
    return jnp.clip(array, min=-most, max=most).astype(kind)


def setup_inputs(seed: int = 0) -> dict:
    seeds = jax.random.split(jax.random.key(seed), 8)
    tokens = scatter_about(seeds[0], (TOKENS, D), 1.0, 6.0, ((0, 8), (1, 128)))
    out_grad = scatter_about(seeds[1], (TOKENS, D), 1.0, 6.0, ((0, 8), (1, 128)))
    expert_ids_keys = jax.random.split(jax.random.fold_in(seeds[2], 1), TOKENS // TOK_NODE)
    expert_ids_turns = jax.random.permutation(jax.random.fold_in(seeds[2], 3), TOKENS // TOK_NODE)
    expert_ids = jax.vmap(lambda own, number: shared_out(jax.random.fold_in(seeds[2], 2), own, number, TOK_NODE, EXPERTS, TOPK, CAP, 2))(expert_ids_keys, expert_ids_turns).reshape((TOKENS, TOPK))
    gate_weights = jnp.clip(jnp.exp(math.log(0.5) - 3.218876 * jax.random.uniform(seeds[3], (TOKENS, TOPK), jnp.float32) ** block_levels(seeds[3], (TOKENS, TOPK), ((0, 8),), -0.2, 0.2)), 0.02, 0.5)
    gate_weight = scatter_about(seeds[4], (EXPERTS * SPLIT, D, HID), D ** -0.5, 0.09375, ((0, 1024),))
    up_weight = scatter_about(seeds[5], (EXPERTS * SPLIT, D, HID), D ** -0.5, 0.09375, ((0, 1024),))
    down_weight = scatter_about(seeds[6], (EXPERTS * SPLIT, HID, D), FF ** -0.5, 0.1875, ((0, 1024),))
    return {"tokens": tokens, "out_grad": out_grad, "expert_ids": expert_ids, "gate_weights": gate_weights, "gate_weight": gate_weight, "up_weight": up_weight, "down_weight": down_weight}


def reference(tokens, out_grad, expert_ids, gate_weights, gate_weight, up_weight, down_weight):
    token_total = tokens.shape[0]
    node_of = (jnp.arange(token_total, dtype=jnp.int32) // TOK_NODE).astype(jnp.int32)
    chosen = jnp.sum((expert_ids[:, :, None] == jnp.arange(EXPERTS, dtype=jnp.int32)[None, None, :]).astype(jnp.int32), axis=1)
    per_node = chosen.reshape(N_NODE, TOK_NODE, EXPERTS)
    before = (jnp.cumsum(per_node, axis=1) - per_node).reshape(token_total, EXPERTS).astype(jnp.int32)
    slot_of = jnp.take_along_axis(before, expert_ids, axis=1).astype(jnp.int32)
    row_ids = jnp.broadcast_to(jnp.arange(token_total, dtype=jnp.int32)[:, None], expert_ids.shape)
    node_ids = jnp.broadcast_to(node_of[:, None], expert_ids.shape)
    row_table = jnp.zeros((EXPERTS, N_NODE, CAP), jnp.int32).at[expert_ids, node_ids, slot_of].set(row_ids)
    filled = jnp.zeros((EXPERTS, N_NODE, CAP), jnp.float32).at[expert_ids, node_ids, slot_of].set(1.0)
    slot_gate = jnp.zeros((EXPERTS, N_NODE, CAP), jnp.float32).at[expert_ids, node_ids, slot_of].set(gate_weights)
    gate_shards = gate_weight.reshape(EXPERTS, SPLIT, D, HID)
    up_shards = up_weight.reshape(EXPERTS, SPLIT, D, HID)
    down_shards = down_weight.reshape(EXPERTS, SPLIT, HID, D)

    def expert_step(grad_acc, inputs):
        row_index, live, scale, gate_mat, up_mat, down_mat = inputs
        flat_index = row_index.reshape(-1)
        live_rows = live.reshape(-1, 1)
        expert_in = (tokens[flat_index].astype(jnp.float32) * live_rows).astype(jnp.bfloat16)
        expert_out = (out_grad[flat_index].astype(jnp.float32) * live_rows).astype(jnp.bfloat16)
        in_wide = expert_in.astype(jnp.float32)
        out_wide = expert_out.astype(jnp.float32)
        gate_wide = gate_mat.astype(jnp.float32)
        up_wide = up_mat.astype(jnp.float32)
        down_wide = down_mat.astype(jnp.float32)
        pre_gate = jnp.einsum('rd,tdh->trh', in_wide, gate_wide)
        pre_up = jnp.einsum('rd,tdh->trh', in_wide, up_wide)
        hidden_grad = jnp.einsum('rd,thd->trh', out_wide, down_wide)
        sigmoid_gate = jax.nn.sigmoid(pre_gate)
        activated = pre_gate * sigmoid_gate
        router_part = jnp.sum(activated * pre_up * hidden_grad, axis=2).astype(jnp.bfloat16)
        up_inner = (hidden_grad * activated).astype(jnp.bfloat16)
        gate_inner = (hidden_grad * pre_up * sigmoid_gate * (1.0 + pre_gate * (1.0 - sigmoid_gate))).astype(jnp.bfloat16)
        partial_value = jnp.einsum('trh,tdh->trd', gate_inner.astype(jnp.float32), gate_wide)
        partial_value = partial_value + jnp.einsum('trh,tdh->trd', up_inner.astype(jnp.float32), up_wide)
        partial_value = partial_value.astype(jnp.bfloat16)
        summed = jnp.sum(partial_value.astype(jnp.float32), axis=0) * scale.reshape(-1, 1)
        grad_acc = grad_acc.at[flat_index].add(summed)
        router_sum = jnp.sum(router_part.astype(jnp.float32), axis=0).reshape(N_NODE, CAP)
        return grad_acc, router_sum

    start = jnp.zeros((token_total, D), jnp.float32)
    grad_acc, router_all = lax.scan(expert_step, start, (row_table, filled, slot_gate, gate_shards, up_shards, down_shards))
    gate_grad = router_all[expert_ids, node_ids, slot_of]
    return grad_acc.astype(jnp.bfloat16), gate_grad
```

```python
import jax
import jax.numpy as jnp
from jax import lax
from jax.experimental import pallas as pl
from jax.experimental.pallas import tpu as pltpu
from jax.sharding import PartitionSpec as P

MESH = pl.DeviceIdType.MESH
F32 = jnp.float32
BF16 = jnp.bfloat16

NODES = 8
GROUP = 16
SHARDS = 8
FEAT = 28
BLOCK = 448
WIDE = 3584
HID = 128
CAP = 16
TOK = 128
TOPK = 8


def dot_nn(left, right):
    return lax.dot_general(left, right, (((1,), (0,)), ((), ())), preferred_element_type=F32)


def dot_nt(left, right):
    return lax.dot_general(left, right, (((1,), (1,)), ((), ())), preferred_element_type=F32)


def split(value):
    high = value.astype(BF16).astype(F32)
    return high, (value - high).astype(BF16).astype(F32)


def kernel(
    tok_ref, grad_ref, ids_ref, gates_ref, wg_hbm, wu_hbm, wd_hbm,
    token_out, gate_out,
    wgu, wgu_t, wd, r1, msg1, select, msg2, r2, xg, ps, pr, pf, ys, yr, msg5, r5, msg6, r6,
    w_sem, s1, v1, s2, v2, s3, v3, s4a, v4a, s4b, v4b, s5, v5, s6, v6,
):
    n = lax.axis_index("node")
    l = lax.axis_index("local")
    col = l // SHARDS
    shard = l % SHARDS
    zz = l // 16
    mm = l % 16
    core = l % 2
    yq = (l // 2) % 4
    sib = l + 1 - 2 * core
    selfish = zz == shard

    loads = [
        pltpu.make_async_copy(wg_hbm.at[0], wgu.at[:, pl.ds(0, HID)], w_sem.at[0]),
        pltpu.make_async_copy(wu_hbm.at[0], wgu.at[:, pl.ds(HID, HID)], w_sem.at[1]),
        pltpu.make_async_copy(wd_hbm.at[0], wd, w_sem.at[2]),
    ]
    for load in loads:
        load.start()

    barrier = pltpu.get_barrier_semaphore()

    def greet(node, local):
        pl.semaphore_signal(barrier, inc=1, device_id=(node, local), device_id_type=MESH)

    for d in range(1, NODES):
        greet((n + d) % NODES, l)
    for d in range(1, 4):
        greet(n, col * 8 + 2 * ((yq + d) % 4) + core)
    greet(n, sib)
    for d in range(1, GROUP):
        greet(n, 8 * ((col + d) % GROUP) + zz)
        greet(n, 16 * shard + (mm + d) % 16)

    @pl.when(jnp.logical_not(selfish))
    def _():
        greet(n, 8 * col + zz)
        greet(n, 16 * shard + mm)

    gates_hi, gates_lo = split(gates_ref[...])
    msg1[...] = jnp.concatenate(
        [
            tok_ref[...].astype(F32),
            grad_ref[...].astype(F32),
            ids_ref[...].astype(F32),
            gates_hi,
            gates_lo,
        ],
        axis=0,
    ).astype(BF16)
    r1[n] = msg1[...]

    pl.semaphore_wait(barrier, 7 + 3 + 1 + 30 + jnp.where(selfish, 0, 2))

    sends = []

    def remote(src, dst, send_sem, recv_sem, local, node=None):
        return pltpu.make_async_remote_copy(
            src_ref=src,
            dst_ref=dst,
            send_sem=send_sem,
            recv_sem=recv_sem,
            device_id=(n if node is None else node, local),
            device_id_type=MESH,
        )

    def send(*args, **kw):
        copy = remote(*args, **kw)
        copy.start()
        sends.append(copy)

    for d in (4, 3, 5, 2, 6, 1, 7):
        send(msg1, r1.at[n], s1.at[d], v1.at[n], l, node=(n + d) % NODES)

    select[...] = jnp.zeros(select.shape, BF16)
    eye = (
        lax.broadcasted_iota(jnp.int32, (256, 256), 0)
        == lax.broadcasted_iota(jnp.int32, (256, 256), 1)
    ).astype(F32).astype(BF16)
    loads[0].wait()
    loads[1].wait()
    for i in range(WIDE // 256):
        wgu_t[:, i * 256 : (i + 1) * 256] = dot_nt(eye, wgu[i * 256 : (i + 1) * 256, :]).astype(BF16)
    loads[2].wait()

    for d in (1, 7, 2, 6, 3, 5, 4):
        j = (n + d) % NODES
        remote(msg1, r1.at[j], s1.at[0], v1.at[j], l).wait_recv()

    base = (n * GROUP).astype(F32)
    expert = lax.broadcasted_iota(jnp.int32, (GROUP, TOK), 0).astype(F32)
    ids = [r1[j, 56:64, :].astype(F32) for j in range(NODES)]
    matched = []
    for j in range(NODES):
        found = jnp.zeros((GROUP, TOK), F32)
        for k in range(TOPK):
            found = jnp.where(ids[j][k : k + 1, :] == expert + base, 1.0, found)
        matched.append(found)
    matched = jnp.concatenate(matched, axis=0)
    before = (
        lax.broadcasted_iota(jnp.int32, (TOK, TOK), 0)
        < lax.broadcasted_iota(jnp.int32, (TOK, TOK), 1)
    ).astype(F32).astype(BF16)
    rank = dot_nn(matched.astype(BF16), before)
    key = jnp.where(matched > 0.0, rank, -1.0)
    slot = lax.broadcasted_iota(jnp.int32, (CAP, TOK), 0).astype(F32)
    for j in range(NODES):
        p, q = j // 2, j % 2
        for c in range(GROUP):
            row = key[j * GROUP + c : j * GROUP + c + 1, :]
            hot = jnp.where(row == slot, 1.0, 0.0).astype(BF16)
            at = ((c % 8) * 2 + q) * CAP
            select[p, c // 8, at : at + CAP, q * TOK : (q + 1) * TOK] = hot

    for h in range(2):
        picked = []
        for p in range(4):
            left = jnp.concatenate([r1[2 * p, 0:64, :], r1[2 * p + 1, 0:64, :]], axis=1)
            picked.append(dot_nt(left, select[p, h]))
        for c in range(8):
            msg2[8 * h + c] = jnp.concatenate(
                [v[:, 32 * c : 32 * c + 32] for v in picked], axis=1
            ).astype(BF16)

    def exchange2(d):
        c = (col + d) % GROUP
        return remote(msg2.at[c], r2.at[mm], s2.at[d], v2.at[mm], 8 * c + zz)

    for d in range(1, GROUP):
        exchange2(d).start()

    @pl.when(jnp.logical_not(selfish))
    def _():
        exchange2(0).start()

    @pl.when(selfish)
    def _():
        r2[mm] = msg2[col]

    own_rows = []
    wanted = base + col.astype(F32)
    for j in range(NODES):
        weights = r1[j, 64:72, :].astype(F32) + r1[j, 72:80, :].astype(F32)
        weight = jnp.sum(jnp.where(ids[j] == wanted, weights, 0.0), axis=0, keepdims=True)
        own_key = jnp.sum(
            jnp.where(expert == col.astype(F32), key[j * GROUP : (j + 1) * GROUP, :], 0.0),
            axis=0,
            keepdims=True,
        )
        own_rows.append(jnp.where(own_key == slot, weight, 0.0))
    own_hi, own_lo = split(jnp.concatenate(own_rows, axis=0))
    ones = jnp.ones((8, TOK), BF16)
    slot_gate = (dot_nt(ones, own_hi.astype(BF16)) + dot_nt(ones, own_lo.astype(BF16)))[0:1, :]

    for d in range(1, GROUP):
        j = (mm + d) % 16
        remote(msg2.at[0], r2.at[j], s2.at[0], v2.at[j], l).wait_recv()

    @pl.when(jnp.logical_not(selfish))
    def _():
        remote(msg2.at[0], r2.at[mm], s2.at[0], v2.at[mm], l).wait_recv()

    for part in range(2):
        for g in range(4):
            rows = jnp.concatenate(
                [r2[4 * g + i, part * FEAT : (part + 1) * FEAT, :].astype(F32) for i in range(4)],
                axis=0,
            )
            at = pl.multiple_of(shard * BLOCK + g * 112, 16)
            xg[part, pl.ds(at, 112), :] = rows.astype(BF16)

    def block(b):
        return xg.at[:, pl.ds(pl.multiple_of(b * BLOCK, 16), BLOCK), :]

    own = block(shard)
    for d in (2, 3, 1):
        peer = (yq + d) % 4
        send(own, own, s3.at[d], v3.at[shard], col * 8 + 2 * peer + core)
    send(own, own, s3.at[4], v3.at[shard], sib)

    acc_gu = jnp.zeros((2 * HID, HID), F32)
    acc_h = jnp.zeros((HID, HID), F32)

    def arrived(b):
        remote(block(b), block(b), s3.at[0], v3.at[b], l).wait_recv()

    for d in range(4):
        q = (yq + d) % 4
        if d < 3:
            mine = 2 * ((yq + d + 1) % 4) + core
            arrived(mine)
            send(block(mine), block(mine), s3.at[5 + d], v3.at[mine], sib)
        arrived(2 * q + 1 - core)
        at = pl.multiple_of(q * 2 * BLOCK, 128)
        acc_gu = acc_gu + dot_nn(wgu_t[:, pl.ds(at, 2 * BLOCK)], xg[0, pl.ds(at, 2 * BLOCK), :])
        acc_h = acc_h + dot_nn(wd[:, pl.ds(at, 2 * BLOCK)], xg[1, pl.ds(at, 2 * BLOCK), :])

    pre_gate, pre_up = acc_gu[:HID], acc_gu[HID:]
    sigmoid = 1.0 / (1.0 + jnp.exp(-pre_gate))
    activated = pre_gate * sigmoid
    router = jnp.sum(activated * pre_up * acc_h, axis=0, keepdims=True)
    up_inner = acc_h * activated
    gate_inner = acc_h * pre_up * sigmoid * (1.0 + pre_gate * (1.0 - sigmoid))
    inner = jnp.concatenate([gate_inner, up_inner], axis=0).astype(BF16)

    def router_rows(value, rows):
        hi, lo = split(value)
        index = lax.broadcasted_iota(jnp.int32, (rows, HID), 0)
        return jnp.where(index == 0, hi, jnp.where(index == 1, lo, 0.0))

    def partial(b):
        return dot_nn(wgu[pl.ds(pl.multiple_of(b * BLOCK, 16), BLOCK), :], inner)

    tail = router_rows(router, 16).astype(BF16)
    for d in (1, 2, 3, 0):
        q = (yq + d) % 4
        ps[d, 0:BLOCK, :] = partial(2 * q + 1 - core).astype(BF16)
        ps[d, BLOCK : BLOCK + 16, :] = tail
        send(ps.at[d], pr.at[d], s4a.at[d], v4a.at[d], sib)
    for d in (1, 2, 3, 0):
        q = (yq + d) % 4
        pf[d] = partial(2 * q + core)
        remote(ps.at[d], pr.at[d], s4a.at[d], v4a.at[d], l).wait_recv()
        if d > 0:
            ys[d, 0:BLOCK, :] = (pf[d] + pr[d, 0:BLOCK, :].astype(F32)).astype(BF16)
            last = pr[d, BLOCK : BLOCK + 16, :].astype(F32)
            both = router + last[0:1, :] + last[1:2, :]
            ys[d, BLOCK : BLOCK + 16, :] = router_rows(both, 16).astype(BF16)
            send(ys.at[d], yr.at[d], s4b.at[d], v4b.at[d], col * 8 + 2 * q + core)
    total = pf[0] + pr[0, 0:BLOCK, :].astype(F32)
    last = pr[0, BLOCK : BLOCK + 16, :].astype(F32)
    router_total = router + last[0:1, :] + last[1:2, :]
    for d in (1, 2, 3):
        remote(ys.at[d], yr.at[d], s4b.at[d], v4b.at[d], l).wait_recv()
        total = total + yr[d, 0:BLOCK, :].astype(F32)
        last = yr[d, BLOCK : BLOCK + 16, :].astype(F32)
        router_total = router_total + last[0:1, :] + last[1:2, :]
    pf[0] = total * slot_gate

    for m in range(16):
        msg5[m] = jnp.concatenate(
            [pf[0, m * FEAT : (m + 1) * FEAT, :], router_rows(router_total, 4)], axis=0
        ).astype(BF16)

    def exchange5(d):
        m = (mm + d) % 16
        return remote(msg5.at[m], r5.at[col], s5.at[d], v5.at[col], 16 * shard + m)

    for d in range(1, 16):
        exchange5(d).start()

    @pl.when(jnp.logical_not(selfish))
    def _():
        exchange5(0).start()

    @pl.when(selfish)
    def _():
        r5[col] = msg5[mm]

    for d in range(1, GROUP):
        j = (col + d) % GROUP
        remote(msg5.at[0], r5.at[j], s5.at[0], v5.at[j], l).wait_recv()

    @pl.when(jnp.logical_not(selfish))
    def _():
        remote(msg5.at[0], r5.at[col], s5.at[0], v5.at[col], l).wait_recv()

    back = [r5[c].astype(F32) for c in range(GROUP)]
    lane = lax.broadcasted_iota(jnp.int32, (8, 256), 1) // 32
    sublane = lax.broadcasted_iota(jnp.int32, (8, 256), 0)
    for p in range(4):
        token_sum = jnp.zeros((32, 256), F32)
        gate_sum = [jnp.zeros((TOPK, TOK), F32) for _ in range(2)]
        for h in range(2):
            rows = jnp.concatenate(
                [back[8 * h + c][:, 32 * p : 32 * p + 32] for c in range(8)], axis=1
            )
            hi = jnp.where(lane == sublane, rows[28:29, :], 0.0)
            lo = jnp.where(lane == sublane, rows[29:30, :], 0.0)
            left = jnp.concatenate([rows, hi, lo], axis=0).astype(BF16)
            out = dot_nn(left, select[p, h])
            token_sum = token_sum + out[0:32]
            routed = out[32:40] + out[40:48]
            for q in range(2):
                for c in range(8):
                    gate_sum[q] = gate_sum[q] + jnp.where(
                        ids[2 * p + q] == base + float(8 * h + c),
                        routed[c : c + 1, q * TOK : (q + 1) * TOK],
                        0.0,
                    )
        for q in range(2):
            msg6[2 * p + q] = jnp.concatenate(
                [token_sum[:, q * TOK : (q + 1) * TOK], gate_sum[q]], axis=0
            )

    for d in (4, 3, 5, 2, 6, 1, 7):
        j = (n + d) % NODES
        send(msg6.at[j], r6.at[n], s6.at[d], v6.at[n], l, node=j)
    result = msg6[n]
    for d in (1, 7, 2, 6, 3, 5, 4):
        j = (n + d) % NODES
        remote(msg6.at[0], r6.at[j], s6.at[0], v6.at[j], l).wait_recv()
        result = result + r6[j]
    token_out[...] = result[0:FEAT].astype(BF16)
    gate_out[...] = result[32:40]

    for copy in sends:
        copy.wait_send()
    for d in range(1, 16):
        exchange2(d).wait_send()
        exchange5(d).wait_send()

    @pl.when(jnp.logical_not(selfish))
    def _():
        exchange2(0).wait_send()
        exchange5(0).wait_send()


def on_device(tokens, out_grad, expert_ids, gate_weights, gate_weight, up_weight, down_weight):
    vmem = pl.BlockSpec(memory_space=pltpu.VMEM)
    anywhere = pl.BlockSpec(memory_space=pl.ANY)
    dma = pltpu.SemaphoreType.DMA
    token_t, gate_t = pl.pallas_call(
        kernel,
        out_shape=(
            jax.ShapeDtypeStruct((FEAT, TOK), BF16),
            jax.ShapeDtypeStruct((TOPK, TOK), F32),
        ),
        in_specs=[vmem] * 4 + [anywhere] * 3,
        out_specs=(vmem, vmem),
        scratch_shapes=[
            pltpu.VMEM((WIDE, 2 * HID), BF16),
            pltpu.VMEM((2 * HID, WIDE), BF16),
            pltpu.VMEM((HID, WIDE), BF16),
            pltpu.VMEM((NODES, 80, TOK), BF16),
            pltpu.VMEM((80, TOK), BF16),
            pltpu.VMEM((4, 2, 256, 256), BF16),
            pltpu.VMEM((GROUP, 64, TOK), BF16),
            pltpu.VMEM((GROUP, 64, TOK), BF16),
            pltpu.VMEM((2, WIDE, TOK), BF16),
            pltpu.VMEM((4, BLOCK + 16, TOK), BF16),
            pltpu.VMEM((4, BLOCK + 16, TOK), BF16),
            pltpu.VMEM((4, BLOCK, TOK), F32),
            pltpu.VMEM((4, BLOCK + 16, TOK), BF16),
            pltpu.VMEM((4, BLOCK + 16, TOK), BF16),
            pltpu.VMEM((16, 32, TOK), BF16),
            pltpu.VMEM((GROUP, 32, TOK), BF16),
            pltpu.VMEM((NODES, 40, TOK), F32),
            pltpu.VMEM((NODES, 40, TOK), F32),
            dma((3,)),
            dma((8,)), dma((8,)),
            dma((16,)), dma((16,)),
            dma((8,)), dma((8,)),
            dma((4,)), dma((4,)),
            dma((4,)), dma((4,)),
            dma((16,)), dma((16,)),
            dma((8,)), dma((8,)),
        ],
        compiler_params=pltpu.CompilerParams(
            collective_id=0, has_side_effects=True, vmem_limit_bytes=40 * 1024 * 1024
        ),
        cost_estimate=pl.CostEstimate(flops=600_000_000, bytes_accessed=3_000_000, transcendentals=16384),
    )(
        tokens.T, out_grad.T, expert_ids.T, gate_weights.T, gate_weight, up_weight, down_weight
    )
    return token_t.T, gate_t.T


def solution(mesh):
    placed = (
        P("node", "local"),
        P("node", "local"),
        P("node", None),
        P("node", None),
        P(("node", "local"), None, None),
        P(("node", "local"), None, None),
        P(("node", "local"), None, None),
    )
    return jax.shard_map(
        on_device,
        mesh=mesh,
        in_specs=placed,
        out_specs=(P("node", "local"), P("node", None)),
        check_vma=False,
    )
```

```python
import jax
import jax.numpy as jnp
from jax import lax
from jax.experimental import pallas as pl
from jax.experimental.pallas import tpu as pltpu
from jax.sharding import PartitionSpec as P

MESH = pl.DeviceIdType.MESH
F32 = jnp.float32
BF16 = jnp.bfloat16

NODES = 8
GROUP = 16
SHARDS = 8
FEAT = 28
BLOCK = 448
HALF = 224
WIDE = 3584
HID = 128
CAP = 16
TOK = 128
TOPK = 8


def dot_nn(left, right):
    return lax.dot_general(left, right, (((1,), (0,)), ((), ())), preferred_element_type=F32)


def dot_nt(left, right):
    return lax.dot_general(left, right, (((1,), (1,)), ((), ())), preferred_element_type=F32)


def split(value):
    high = value.astype(BF16).astype(F32)
    return high, (value - high).astype(BF16).astype(F32)


def shard_of(delta, half):
    far = delta // 4
    q = (1 - far) * delta + far * ((8 - delta) % 4)
    return 2 * (q + half * (1 - 2 * (q % 2))) + far


def plane_of(q, core, half):
    q = q + half * (1 - 2 * (q % 2))
    return (1 - core) * q + core * (4 + (4 - q) % 4)


def pick(index, *options):
    out = options[0]
    for i in range(1, len(options)):
        out = jnp.where(index == i, options[i], out)
    return out


def kernel(
    tok_hbm, grad_hbm, ids_hbm, gates_hbm, wg_hbm, wu_hbm, wd_hbm,
    token_out, gate_out,
    tok_ref, grad_ref, ids_ref, gates_ref,
    wgu, wgu_t, wd, wd_b, r1, msg1, select, msg2, r2, xg, ps, pr, pf, ys, yr, yrel, msg5, r5, msg6, r6,
    w_sem, s1, v1, s2, v2, s3, v3y, v3s, s4a, v4a, s4b, v4b, vrel, s5, v5, s6, v6,
):
    n = lax.axis_index("node")
    l = lax.axis_index("local")
    col = l // SHARDS
    zz = l // 16
    mm = l % 16
    half_me = col % 2
    core = l % 2
    yq = (l // 2) % 4
    sib = l + 1 - 2 * core
    mid = (yq == 1) | (yq == 2)
    outer = (yq == 0) | (yq == 3)
    z_near = (zz + plane_of(yq, core, 0)) % 8
    z_far = (zz + plane_of(yq, core, 1)) % 8

    def home(m):
        return 16 * (z_near + (m // 8) * (z_far - z_near)) + m

    def gatherer(c):
        return 8 * c + shard_of((zz - c // 2 + 8) % 8, half_me)

    selfish = l % 8 == 2 * half_me

    loads = [
        pltpu.make_async_copy(tok_hbm, tok_ref, w_sem.at[0]),
        pltpu.make_async_copy(grad_hbm, grad_ref, w_sem.at[1]),
        pltpu.make_async_copy(ids_hbm, ids_ref, w_sem.at[2]),
        pltpu.make_async_copy(gates_hbm, gates_ref, w_sem.at[3]),
        pltpu.make_async_copy(wg_hbm.at[0], wgu.at[:, pl.ds(0, HID)], w_sem.at[4]),
        pltpu.make_async_copy(wu_hbm.at[0], wgu.at[:, pl.ds(HID, HID)], w_sem.at[5]),
        pltpu.make_async_copy(wd_hbm.at[0], wd, w_sem.at[6]),
    ]
    for load in loads:
        load.start()

    barrier = pltpu.get_barrier_semaphore()

    def greet(node, local):
        pl.semaphore_signal(barrier, inc=1, device_id=(node, local), device_id_type=MESH)

    for d in range(1, NODES):
        greet((n + d) % NODES, l)
    for d in range(1, 4):
        greet(n, col * 8 + 2 * ((yq + d) % 4) + core)
    greet(n, sib)
    for d in range(1, GROUP):
        greet(n, gatherer((col + d) % GROUP))
        greet(n, home((mm + d) % 16))

    @pl.when(jnp.logical_not(selfish))
    def _():
        greet(n, gatherer(col))
        greet(n, home(mm))

    for load in loads[:4]:
        load.wait()
    gates_hi, gates_lo = split(gates_ref[...])
    msg1[...] = jnp.concatenate(
        [
            tok_ref[...].astype(F32),
            grad_ref[...].astype(F32),
            ids_ref[...].astype(F32),
            gates_hi,
            gates_lo,
        ],
        axis=0,
    ).astype(BF16)
    r1[n] = msg1[...]

    pl.semaphore_wait(barrier, 7 + 3 + 1 + 30 + jnp.where(selfish, 0, 2))

    sends = []

    def remote(src, dst, send_sem, recv_sem, local, node=None):
        return pltpu.make_async_remote_copy(
            src_ref=src,
            dst_ref=dst,
            send_sem=send_sem,
            recv_sem=recv_sem,
            device_id=(n if node is None else node, local),
            device_id_type=MESH,
        )

    def send(*args, **kw):
        copy = remote(*args, **kw)
        copy.start()
        sends.append(copy)

    for d in (4, 3, 5, 2, 6, 1, 7):
        send(msg1, r1.at[n], s1.at[d], v1.at[n], l, node=(n + d) % NODES)

    select[...] = jnp.zeros(select.shape, BF16)
    eye = (
        lax.broadcasted_iota(jnp.int32, (256, 256), 0)
        == lax.broadcasted_iota(jnp.int32, (256, 256), 1)
    ).astype(F32).astype(BF16)
    loads[4].wait()
    loads[5].wait()
    for i in range(16):
        wgu_t[i] = dot_nt(eye, wgu[i * HALF : (i + 1) * HALF, :]).astype(BF16)
    loads[6].wait()
    for i in range(16):
        wd_b[i] = wd[:, i * HALF : (i + 1) * HALF]

    for d in (1, 7, 2, 6, 3, 5, 4):
        j = (n + d) % NODES
        remote(msg1, r1.at[j], s1.at[0], v1.at[j], l).wait_recv()

    base = (n * GROUP).astype(F32)
    expert = lax.broadcasted_iota(jnp.int32, (GROUP, TOK), 0).astype(F32)
    ids = [r1[j, 56:64, :].astype(F32) for j in range(NODES)]
    matched = []
    for j in range(NODES):
        found = jnp.zeros((GROUP, TOK), F32)
        for k in range(TOPK):
            found = jnp.where(ids[j][k : k + 1, :] == expert + base, 1.0, found)
        matched.append(found)
    matched = jnp.concatenate(matched, axis=0)
    before = (
        lax.broadcasted_iota(jnp.int32, (TOK, TOK), 0)
        < lax.broadcasted_iota(jnp.int32, (TOK, TOK), 1)
    ).astype(F32).astype(BF16)
    rank = dot_nn(matched.astype(BF16), before)
    key = jnp.where(matched > 0.0, rank, -1.0)
    slot = lax.broadcasted_iota(jnp.int32, (CAP, TOK), 0).astype(F32)
    for j in range(NODES):
        p, q = j // 2, j % 2
        for c in range(GROUP):
            row = key[j * GROUP + c : j * GROUP + c + 1, :]
            hot = jnp.where(row == slot, 1.0, 0.0).astype(BF16)
            at = ((c % 8) * 2 + q) * CAP
            select[p, c // 8, at : at + CAP, q * TOK : (q + 1) * TOK] = hot

    for h in range(2):
        picked = []
        for p in range(4):
            left = jnp.concatenate([r1[2 * p, 0:64, :], r1[2 * p + 1, 0:64, :]], axis=1)
            picked.append(dot_nt(left, select[p, h]))
        for c in range(8):
            msg2[8 * h + c] = jnp.concatenate(
                [v[:, 32 * c : 32 * c + 32] for v in picked], axis=1
            ).astype(BF16)

    def exchange2(d):
        c = (col + d) % GROUP
        return remote(msg2.at[c], r2.at[mm], s2.at[d], v2.at[mm], gatherer(c))

    for d in range(1, GROUP):
        exchange2(d).start()

    @pl.when(jnp.logical_not(selfish))
    def _():
        exchange2(0).start()

    @pl.when(selfish)
    def _():
        r2[mm] = msg2[col]

    own_rows = []
    wanted = base + col.astype(F32)
    for j in range(NODES):
        weights = r1[j, 64:72, :].astype(F32) + r1[j, 72:80, :].astype(F32)
        weight = jnp.sum(jnp.where(ids[j] == wanted, weights, 0.0), axis=0, keepdims=True)
        own_key = jnp.sum(
            jnp.where(expert == col.astype(F32), key[j * GROUP : (j + 1) * GROUP, :], 0.0),
            axis=0,
            keepdims=True,
        )
        own_rows.append(jnp.where(own_key == slot, weight, 0.0))
    own_hi, own_lo = split(jnp.concatenate(own_rows, axis=0))
    ones = jnp.ones((8, TOK), BF16)
    slot_gate = (dot_nt(ones, own_hi.astype(BF16)) + dot_nt(ones, own_lo.astype(BF16)))[0:1, :]

    def half_at(q, k, h):
        return pl.ds(pl.multiple_of((2 * ((zz + plane_of(q, k, h)) % 8) + h) * HALF, 16), HALF)

    def piece(q, k, h):
        return xg.at[:, half_at(q, k, h), :]

    def mate(q):
        return col * 8 + 2 * q + core

    relay_to = 3 * (yq - 1)
    towards = ((2, 1), (3, 0, 2), (0, 3, 1), (1, 2))
    y_sends = [[], [], [], []]

    def gathered(m):
        remote(msg2.at[0], r2.at[m], s2.at[0], v2.at[m], l).wait_recv()

    for h in range(2):
        for i in range(8):
            m = 8 * h + i

            @pl.when(jnp.logical_not(selfish & (mm == m)))
            def _():
                gathered(m)

        for part in range(2):
            for g in range(2):
                rows = jnp.concatenate(
                    [
                        r2[8 * h + 4 * g + i, part * FEAT : (part + 1) * FEAT, :].astype(F32)
                        for i in range(4)
                    ],
                    axis=0,
                ).astype(BF16)
                at = (2 * (z_near + h * (z_far - z_near)) + h) * HALF + g * 112
                xg[part, pl.ds(pl.multiple_of(at, 16), 112), :] = rows
        own = piece(yq, core, h)
        for s in range(4):

            @pl.when(yq == s)
            def _():
                for i, p in enumerate(towards[s]):
                    copy = remote(own, own, s3.at[2 * i + h], v3y.at[2 * s + h], mate(p))
                    copy.start()
                    y_sends[s].append(copy)

        send(own, own, s3.at[6 + h], v3s.at[2 * yq + h], sib)

    acc_gu = jnp.zeros((2 * HID, HID), F32)
    acc_h = jnp.zeros((HID, HID), F32)
    order3 = [pick(yq, 1, 3, 0, 2), pick(yq, 2, 0, 3, 1), pick(yq, 3, 2, 1, 0)]

    def add_piece(acc, q, k, h):
        b = 2 * ((zz + plane_of(q, k, h)) % 8) + h
        rows = half_at(q, k, h)
        return acc[0] + dot_nn(wgu_t[b], xg[0, rows, :]), acc[1] + dot_nn(wd_b[b], xg[1, rows, :])

    acc = (acc_gu, acc_h)

    def from_sibling(acc, q, h):
        there = piece(q, 1 - core, h)
        remote(there, there, s3.at[0], v3s.at[2 * q + h], l).wait_recv()
        return add_piece(acc, q, 1 - core, h)

    for h in range(2):
        acc = add_piece(acc, yq, core, h)
    for h in range(2):
        for i in range(3):
            q = order3[i]
            there = piece(q, core, h)
            remote(there, there, s3.at[0], v3y.at[2 * q + h], l).wait_recv()
            send(there, there, s3.at[8 + 2 * i + h], v3s.at[2 * q + h], sib)
            if i == 0:

                @pl.when(mid)
                def _():
                    remote(there, there, s3.at[14 + h], v3y.at[2 * q + h], mate(relay_to)).start()

            acc = add_piece(acc, q, core, h)
            acc = from_sibling(acc, yq if i == 0 else order3[i - 1], h)
        acc = from_sibling(acc, order3[2], h)
    acc_gu, acc_h = acc

    pre_gate, pre_up = acc_gu[:HID], acc_gu[HID:]
    sigmoid = 1.0 / (1.0 + jnp.exp(-pre_gate))
    activated = pre_gate * sigmoid
    router = jnp.sum(activated * pre_up * acc_h, axis=0, keepdims=True)
    up_inner = acc_h * activated
    gate_inner = acc_h * pre_up * sigmoid * (1.0 + pre_gate * (1.0 - sigmoid))
    inner = jnp.concatenate([gate_inner, up_inner], axis=0).astype(BF16)

    def router_rows(value, rows):
        hi, lo = split(value)
        index = lax.broadcasted_iota(jnp.int32, (rows, HID), 0)
        return jnp.where(index == 0, hi, jnp.where(index == 1, lo, 0.0))

    def partial(q, k, h):
        return dot_nn(wgu[half_at(q, k, h), :], inner)

    order4 = [pick(yq, 3, 2, 1, 0), pick(yq, 2, 0, 3, 1), pick(yq, 1, 3, 0, 2), yq]
    tail = router_rows(router, 16).astype(BF16)
    for i in range(4):
        for h in range(2):
            ps[i, h * HALF : (h + 1) * HALF, :] = partial(order4[i], 1 - core, h).astype(BF16)
        ps[i, BLOCK : BLOCK + 16, :] = tail
        send(ps.at[i], pr.at[i], s4a.at[i], v4a.at[i], sib)

    def add_in(i, buf):
        pf[i, 0:BLOCK, :] += buf[0:BLOCK, :].astype(F32)
        last = buf[BLOCK : BLOCK + 16, :].astype(F32)
        pf[i, BLOCK : BLOCK + 8, :] += last[0:1, :] + last[1:2, :]

    for i in range(4):
        for h in range(2):
            pf[i, h * HALF : (h + 1) * HALF, :] = partial(order4[i], core, h)
        pf[i, BLOCK : BLOCK + 8, :] = jnp.broadcast_to(router, (8, HID))
        remote(ps.at[i], pr.at[i], s4a.at[i], v4a.at[i], l).wait_recv()
        add_in(i, pr.at[i])
        if i == 2:

            @pl.when(mid)
            def _():
                remote(ys.at[0], yrel, s4b.at[0], vrel.at[0], l).wait_recv()
                add_in(2, yrel)

        if i < 3:
            ys[i, 0:BLOCK, :] = pf[i, 0:BLOCK, :].astype(BF16)
            ys[i, BLOCK : BLOCK + 16, :] = router_rows(pf[i, BLOCK : BLOCK + 1, :], 16).astype(BF16)
            direct = remote(ys.at[i], yr.at[yq], s4b.at[i], v4b.at[yq], mate(order4[i]))
            if i == 0:

                @pl.when(mid)
                def _():
                    direct.start()

                @pl.when(outer)
                def _():
                    remote(ys.at[0], yrel, s4b.at[0], vrel.at[0], mate(1 + yq // 3)).start()

            else:
                direct.start()
            sends.append(direct)
    for s in range(4):
        absent = (yq == s) | (yq == 3 - s) if s in (0, 3) else yq == s

        @pl.when(jnp.logical_not(absent))
        def _():
            remote(ys.at[0], yr.at[s], s4b.at[0], v4b.at[s], l).wait_recv()
            add_in(3, yr.at[s])

    router_total = pf[3, BLOCK : BLOCK + 1, :]

    for m in range(16):
        msg5[m] = jnp.concatenate(
            [pf[3, m * FEAT : (m + 1) * FEAT, :] * slot_gate, router_rows(router_total, 4)], axis=0
        ).astype(BF16)

    def exchange5(d):
        m = (mm + d) % 16
        return remote(msg5.at[m], r5.at[col], s5.at[d], v5.at[col], home(m))

    for d in range(1, 16):
        exchange5(d).start()

    @pl.when(jnp.logical_not(selfish))
    def _():
        exchange5(0).start()

    @pl.when(selfish)
    def _():
        r5[col] = msg5[mm]

    for d in range(1, GROUP):
        j = (col + d) % GROUP
        remote(msg5.at[0], r5.at[j], s5.at[0], v5.at[j], l).wait_recv()

    @pl.when(jnp.logical_not(selfish))
    def _():
        remote(msg5.at[0], r5.at[col], s5.at[0], v5.at[col], l).wait_recv()

    back = [r5[c].astype(F32) for c in range(GROUP)]
    lane = lax.broadcasted_iota(jnp.int32, (8, 256), 1) // 32
    sublane = lax.broadcasted_iota(jnp.int32, (8, 256), 0)
    for p in range(4):
        token_sum = jnp.zeros((32, 256), F32)
        gate_sum = [jnp.zeros((TOPK, TOK), F32) for _ in range(2)]
        for h in range(2):
            rows = jnp.concatenate(
                [back[8 * h + c][:, 32 * p : 32 * p + 32] for c in range(8)], axis=1
            )
            hi = jnp.where(lane == sublane, rows[28:29, :], 0.0)
            lo = jnp.where(lane == sublane, rows[29:30, :], 0.0)
            left = jnp.concatenate([rows, hi, lo], axis=0).astype(BF16)
            out = dot_nn(left, select[p, h])
            token_sum = token_sum + out[0:32]
            routed = out[32:40] + out[40:48]
            for q in range(2):
                for c in range(8):
                    gate_sum[q] = gate_sum[q] + jnp.where(
                        ids[2 * p + q] == base + float(8 * h + c),
                        routed[c : c + 1, q * TOK : (q + 1) * TOK],
                        0.0,
                    )
        for q in range(2):
            msg6[2 * p + q] = jnp.concatenate(
                [token_sum[:, q * TOK : (q + 1) * TOK], gate_sum[q]], axis=0
            )

    for d in (4, 3, 5, 2, 6, 1, 7):
        j = (n + d) % NODES
        send(msg6.at[j], r6.at[n], s6.at[d], v6.at[n], l, node=j)
    result = msg6[n]
    for d in (1, 7, 2, 6, 3, 5, 4):
        j = (n + d) % NODES
        remote(msg6.at[0], r6.at[j], s6.at[0], v6.at[j], l).wait_recv()
        result = result + r6[j]
    token_out[...] = result[0:FEAT].astype(BF16)
    gate_out[...] = result[32:40]

    for copy in sends:
        copy.wait_send()
    for d in range(1, 16):
        exchange2(d).wait_send()
        exchange5(d).wait_send()

    @pl.when(jnp.logical_not(selfish))
    def _():
        exchange2(0).wait_send()
        exchange5(0).wait_send()

    for s in range(4):

        @pl.when(yq == s)
        def _():
            for i in range(len(towards[s])):
                for h in range(2):
                    own = piece(yq, core, h)
                    remote(own, own, s3.at[2 * i + h], v3y.at[0], l).wait_send()

    @pl.when(mid)
    def _():
        for h in range(2):
            there = piece(order3[0], core, h)
            remote(there, there, s3.at[14 + h], v3y.at[0], l).wait_send()


def on_device(tokens, out_grad, expert_ids, gate_weights, gate_weight, up_weight, down_weight):
    vmem = pl.BlockSpec(memory_space=pltpu.VMEM)
    hbm = pl.BlockSpec(memory_space=pltpu.HBM)
    dma = pltpu.SemaphoreType.DMA
    token_t, gate_t = pl.pallas_call(
        kernel,
        out_shape=(
            jax.ShapeDtypeStruct((FEAT, TOK), BF16),
            jax.ShapeDtypeStruct((TOPK, TOK), F32),
        ),
        in_specs=[hbm] * 7,
        out_specs=(vmem, vmem),
        scratch_shapes=[
            pltpu.VMEM((FEAT, TOK), BF16),
            pltpu.VMEM((FEAT, TOK), BF16),
            pltpu.VMEM((TOPK, TOK), jnp.int32),
            pltpu.VMEM((TOPK, TOK), F32),
            pltpu.VMEM((WIDE, 2 * HID), BF16),
            pltpu.VMEM((16, 2 * HID, HALF), BF16),
            pltpu.VMEM((HID, WIDE), BF16),
            pltpu.VMEM((16, HID, HALF), BF16),
            pltpu.VMEM((NODES, 80, TOK), BF16),
            pltpu.VMEM((80, TOK), BF16),
            pltpu.VMEM((4, 2, 256, 256), BF16),
            pltpu.VMEM((GROUP, 64, TOK), BF16),
            pltpu.VMEM((GROUP, 64, TOK), BF16),
            pltpu.VMEM((2, WIDE, TOK), BF16),
            pltpu.VMEM((4, BLOCK + 16, TOK), BF16),
            pltpu.VMEM((4, BLOCK + 16, TOK), BF16),
            pltpu.VMEM((4, BLOCK + 8, TOK), F32),
            pltpu.VMEM((4, BLOCK + 16, TOK), BF16),
            pltpu.VMEM((4, BLOCK + 16, TOK), BF16),
            pltpu.VMEM((BLOCK + 16, TOK), BF16),
            pltpu.VMEM((16, 32, TOK), BF16),
            pltpu.VMEM((GROUP, 32, TOK), BF16),
            pltpu.VMEM((NODES, 40, TOK), F32),
            pltpu.VMEM((NODES, 40, TOK), F32),
            dma((7,)),
            dma((8,)), dma((8,)),
            dma((16,)), dma((16,)),
            dma((16,)), dma((8,)), dma((8,)),
            dma((4,)), dma((4,)),
            dma((4,)), dma((4,)), dma((1,)),
            dma((16,)), dma((16,)),
            dma((8,)), dma((8,)),
        ],
        compiler_params=pltpu.CompilerParams(
            collective_id=0, has_side_effects=True, vmem_limit_bytes=64 * 1024 * 1024
        ),
        cost_estimate=pl.CostEstimate(flops=600_000_000, bytes_accessed=3_000_000, transcendentals=16384),
    )(
        tokens.T, out_grad.T, expert_ids.T, gate_weights.T, gate_weight, up_weight, down_weight
    )
    return token_t.T, gate_t.T


def solution(mesh):
    placed = (
        P("node", "local"),
        P("node", "local"),
        P("node", None),
        P("node", None),
        P(("node", "local"), None, None),
        P(("node", "local"), None, None),
        P(("node", "local"), None, None),
    )
    return jax.shard_map(
        on_device,
        mesh=mesh,
        in_specs=placed,
        out_specs=(P("node", "local"), P("node", None)),
        check_vma=False,
    )
```

```python
import jax
import jax.numpy as jnp
from jax import lax
from jax.experimental import pallas as pl
from jax.experimental.pallas import tpu as pltpu
from jax.sharding import PartitionSpec as P

MESH = pl.DeviceIdType.MESH
F32 = jnp.float32
BF16 = jnp.bfloat16

NODES = 8
GROUP = 16
SHARDS = 8
FEAT = 28
BLOCK = 448
HALF = 224
WIDE = 3584
HID = 128
CAP = 16
TOK = 128
TOPK = 8
FAR_FIRST = (8, 7, 9, 6, 10, 5, 11, 4, 12, 3, 13, 2, 14, 1, 15)


def dot_nn(left, right):
    return lax.dot_general(left, right, (((1,), (0,)), ((), ())), preferred_element_type=F32)


def dot_nt(left, right):
    return lax.dot_general(left, right, (((1,), (1,)), ((), ())), preferred_element_type=F32)


def split(value):
    high = value.astype(BF16).astype(F32)
    return high, (value - high).astype(BF16).astype(F32)


def shard_of(delta, half):
    far = lax.div(delta, 4)
    q = (1 - far) * delta + far * lax.rem(8 - delta, 4)
    return 2 * (q + half * (1 - 2 * lax.rem(q, 2))) + far


def plane_of(q, core, half):
    q = q + half * (1 - 2 * lax.rem(q, 2))
    return (1 - core) * q + core * (4 + lax.rem(4 - q, 4))


def pick(index, *options):
    out = options[0]
    for i in range(1, len(options)):
        out = jnp.where(index == i, options[i], out)
    return out


def kernel(
    tok_hbm, grad_hbm, ids_hbm, gates_hbm, wg_hbm, wu_hbm, wd_hbm,
    token_out, gate_out,
    tok_ref, grad_ref, ids_ref, gates_ref,
    wgu, wgu_t, wd, wd_b, r1, msg1, select, msg2, r2, xg, ps, pr, pf, ys, yr, yrel, msg5, r5, msg6, r6,
    w_sem, s1, v1, s2, v2, s3, v3y, v3s, s4a, v4a, s4b, v4b, vrel, s5, v5, s6, v6,
):
    n = lax.axis_index("node")
    l = lax.axis_index("local")
    col = lax.div(l, SHARDS)
    zz = lax.div(l, 16)
    mm = lax.rem(l, 16)
    half_me = lax.rem(col, 2)
    core = lax.rem(l, 2)
    yq = lax.rem(lax.div(l, 2), 4)
    sib = l + 1 - 2 * core
    mid = (yq == 1) | (yq == 2)
    outer = (yq == 0) | (yq == 3)
    z_near = lax.rem(zz + plane_of(yq, core, 0), 8)
    z_far = lax.rem(zz + plane_of(yq, core, 1), 8)

    def home(m):
        later = m // 8 if isinstance(m, int) else lax.div(m, 8)
        return 16 * (z_near + later * (z_far - z_near)) + m

    def gatherer(c):
        return 8 * c + shard_of(lax.rem(zz - lax.div(c, 2) + 8, 8), half_me)

    selfish = lax.rem(l, 8) == 2 * half_me

    loads = [
        pltpu.make_async_copy(tok_hbm, tok_ref, w_sem.at[0]),
        pltpu.make_async_copy(grad_hbm, grad_ref, w_sem.at[1]),
        pltpu.make_async_copy(ids_hbm, ids_ref, w_sem.at[2]),
        pltpu.make_async_copy(gates_hbm, gates_ref, w_sem.at[3]),
        pltpu.make_async_copy(wg_hbm.at[0], wgu.at[:, pl.ds(0, HID)], w_sem.at[4]),
        pltpu.make_async_copy(wu_hbm.at[0], wgu.at[:, pl.ds(HID, HID)], w_sem.at[5]),
        pltpu.make_async_copy(wd_hbm.at[0], wd, w_sem.at[6]),
    ]
    for load in loads:
        load.start()

    barrier = pltpu.get_barrier_semaphore()

    def greet(node, local):
        pl.semaphore_signal(barrier, inc=1, device_id=(node, local), device_id_type=MESH)

    for d in range(1, NODES):
        greet(lax.rem(n + d, NODES), l)
    for d in range(1, 4):
        greet(n, col * 8 + 2 * (lax.rem(yq + d, 4)) + core)
    greet(n, sib)
    for d in range(1, GROUP):
        greet(n, gatherer(lax.rem(col + d, GROUP)))
        greet(n, home(lax.rem(mm + d, 16)))

    @pl.when(jnp.logical_not(selfish))
    def _():
        greet(n, gatherer(col))
        greet(n, home(mm))

    for load in loads[:4]:
        load.wait()
    gates_hi, gates_lo = split(gates_ref[...])
    msg1[...] = jnp.concatenate(
        [
            tok_ref[...].astype(F32),
            grad_ref[...].astype(F32),
            ids_ref[...].astype(F32),
            gates_hi,
            gates_lo,
        ],
        axis=0,
    ).astype(BF16)
    r1[n] = msg1[...]

    pl.semaphore_wait(barrier, 7 + 3 + 1 + 30 + jnp.where(selfish, 0, 2))

    sends = []

    def remote(src, dst, send_sem, recv_sem, local, node=None):
        return pltpu.make_async_remote_copy(
            src_ref=src,
            dst_ref=dst,
            send_sem=send_sem,
            recv_sem=recv_sem,
            device_id=(n if node is None else node, local),
            device_id_type=MESH,
        )

    def send(*args, **kw):
        copy = remote(*args, **kw)
        copy.start()
        sends.append(copy)

    for d in (4, 3, 5, 2, 6, 1, 7):
        send(msg1, r1.at[n], s1.at[d], v1.at[n], l, node=lax.rem(n + d, NODES))

    select[...] = jnp.zeros(select.shape, BF16)
    eye = (
        lax.broadcasted_iota(jnp.int32, (256, 256), 0)
        == lax.broadcasted_iota(jnp.int32, (256, 256), 1)
    ).astype(F32).astype(BF16)
    loads[4].wait()
    loads[5].wait()
    for i in range(16):
        wgu_t[i] = dot_nt(eye, wgu[i * HALF : (i + 1) * HALF, :]).astype(BF16)
    loads[6].wait()
    for i in range(16):
        wd_b[i] = wd[:, i * HALF : (i + 1) * HALF]

    for d in (1, 7, 2, 6, 3, 5, 4):
        j = lax.rem(n + d, NODES)
        remote(msg1, r1.at[j], s1.at[0], v1.at[j], l).wait_recv()

    base = (n * GROUP).astype(F32)
    expert = lax.broadcasted_iota(jnp.int32, (GROUP, TOK), 0).astype(F32)
    ids = [r1[j, 56:64, :].astype(F32) for j in range(NODES)]
    matched = []
    for j in range(NODES):
        found = jnp.zeros((GROUP, TOK), F32)
        for k in range(TOPK):
            found = jnp.where(ids[j][k : k + 1, :] == expert + base, 1.0, found)
        matched.append(found)
    matched = jnp.concatenate(matched, axis=0)
    before = (
        lax.broadcasted_iota(jnp.int32, (TOK, TOK), 0)
        < lax.broadcasted_iota(jnp.int32, (TOK, TOK), 1)
    ).astype(F32).astype(BF16)
    rank = dot_nn(matched.astype(BF16), before)
    key = jnp.where(matched > 0.0, rank, -1.0)
    slot = lax.broadcasted_iota(jnp.int32, (CAP, TOK), 0).astype(F32)
    for j in range(NODES):
        p, q = j // 2, j % 2
        for c in range(GROUP):
            row = key[j * GROUP + c : j * GROUP + c + 1, :]
            hot = jnp.where(row == slot, 1.0, 0.0).astype(BF16)
            at = ((c % 8) * 2 + q) * CAP
            select[p, c // 8, at : at + CAP, q * TOK : (q + 1) * TOK] = hot

    for h in range(2):
        picked = []
        for p in range(4):
            left = jnp.concatenate([r1[2 * p, 0:64, :], r1[2 * p + 1, 0:64, :]], axis=1)
            picked.append(dot_nt(left, select[p, h]))
        for c in range(8):
            msg2[8 * h + c] = jnp.concatenate(
                [v[:, 32 * c : 32 * c + 32] for v in picked], axis=1
            ).astype(BF16)

    def exchange2(d):
        c = lax.rem(col + d, GROUP)
        return remote(msg2.at[c], r2.at[mm], s2.at[d], v2.at[mm], gatherer(c))

    for d in FAR_FIRST:
        exchange2(d).start()

    @pl.when(jnp.logical_not(selfish))
    def _():
        exchange2(0).start()

    @pl.when(selfish)
    def _():
        r2[mm] = msg2[col]

    own_rows = []
    wanted = base + col.astype(F32)
    for j in range(NODES):
        weights = r1[j, 64:72, :].astype(F32) + r1[j, 72:80, :].astype(F32)
        weight = jnp.sum(jnp.where(ids[j] == wanted, weights, 0.0), axis=0, keepdims=True)
        own_key = jnp.sum(
            jnp.where(expert == col.astype(F32), key[j * GROUP : (j + 1) * GROUP, :], 0.0),
            axis=0,
            keepdims=True,
        )
        own_rows.append(jnp.where(own_key == slot, weight, 0.0))
    own_hi, own_lo = split(jnp.concatenate(own_rows, axis=0))
    ones = jnp.ones((8, TOK), BF16)
    slot_gate = (dot_nt(ones, own_hi.astype(BF16)) + dot_nt(ones, own_lo.astype(BF16)))[0:1, :]

    def half_at(q, k, h):
        return pl.ds(pl.multiple_of((2 * lax.rem(zz + plane_of(q, k, h), 8) + h) * HALF, 16), HALF)

    def piece(q, k, h):
        return xg.at[:, half_at(q, k, h), :]

    def mate(q):
        return col * 8 + 2 * q + core

    relay_to = 3 * (yq - 1)
    soon = ((2,), (3, 0), (0, 3), (1,))
    later = (1, 2, 1, 2)

    def gathered(m):
        remote(msg2.at[0], r2.at[m], s2.at[0], v2.at[m], l).wait_recv()

    for h in range(2):
        for i in range(8):
            m = 8 * h + i

            @pl.when(jnp.logical_not(selfish & (mm == m)))
            def _():
                gathered(m)

        for part in range(2):
            for g in range(2):
                rows = jnp.concatenate(
                    [
                        r2[8 * h + 4 * g + i, part * FEAT : (part + 1) * FEAT, :].astype(F32)
                        for i in range(4)
                    ],
                    axis=0,
                ).astype(BF16)
                at = (2 * (z_near + h * (z_far - z_near)) + h) * HALF + g * 112
                xg[part, pl.ds(pl.multiple_of(at, 16), 112), :] = rows
        own = piece(yq, core, h)
        for s in range(4):

            @pl.when(yq == s)
            def _():
                for i, p in enumerate(soon[s]):
                    remote(own, own, s3.at[2 * i + h], v3y.at[2 * s + h], mate(p)).start()

        send(own, own, s3.at[6 + h], v3s.at[2 * yq + h], sib)

    for s in range(4):

        @pl.when(yq == s)
        def _():
            for h in range(2):
                own = piece(yq, core, h)
                remote(own, own, s3.at[4 + h], v3y.at[2 * s + h], mate(later[s])).start()

    acc_gu = jnp.zeros((2 * HID, HID), F32)
    acc_h = jnp.zeros((HID, HID), F32)
    order3 = [pick(yq, 1, 3, 0, 2), pick(yq, 2, 0, 3, 1), pick(yq, 3, 2, 1, 0)]

    def add_piece(acc, q, k, h):
        b = 2 * lax.rem(zz + plane_of(q, k, h), 8) + h
        rows = half_at(q, k, h)
        return acc[0] + dot_nn(wgu_t[b], xg[0, rows, :]), acc[1] + dot_nn(wd_b[b], xg[1, rows, :])

    acc = (acc_gu, acc_h)

    def from_sibling(acc, q, h):
        there = piece(q, 1 - core, h)
        remote(there, there, s3.at[0], v3s.at[2 * q + h], l).wait_recv()
        return add_piece(acc, q, 1 - core, h)

    for h in range(2):
        acc = add_piece(acc, yq, core, h)
    for i in range(3):
        q = order3[i]
        for h in range(2):
            there = piece(q, core, h)
            remote(there, there, s3.at[0], v3y.at[2 * q + h], l).wait_recv()
            if i == 0:

                @pl.when(mid)
                def _():
                    remote(there, there, s3.at[14 + h], v3y.at[2 * q + h], mate(relay_to)).start()

            send(there, there, s3.at[8 + 2 * i + h], v3s.at[2 * q + h], sib)
            acc = add_piece(acc, q, core, h)
            acc = from_sibling(acc, yq if i == 0 else order3[i - 1], h)
    for h in range(2):
        acc = from_sibling(acc, order3[2], h)
    acc_gu, acc_h = acc

    pre_gate, pre_up = acc_gu[:HID], acc_gu[HID:]
    sigmoid = 1.0 / (1.0 + jnp.exp(-pre_gate))
    activated = pre_gate * sigmoid
    router = jnp.sum(activated * pre_up * acc_h, axis=0, keepdims=True)
    up_inner = acc_h * activated
    gate_inner = acc_h * pre_up * sigmoid * (1.0 + pre_gate * (1.0 - sigmoid))
    inner = jnp.concatenate([gate_inner, up_inner], axis=0).astype(BF16)

    def router_rows(value, rows):
        hi, lo = split(value)
        index = lax.broadcasted_iota(jnp.int32, (rows, HID), 0)
        return jnp.where(index == 0, hi, jnp.where(index == 1, lo, 0.0))

    def partial(q, k, h):
        return dot_nn(wgu[half_at(q, k, h), :], inner)

    order4 = [pick(yq, 3, 2, 1, 0), pick(yq, 2, 0, 3, 1), pick(yq, 1, 3, 0, 2), yq]
    tail = router_rows(router, 16).astype(BF16)
    for i in range(4):
        for h in range(2):
            ps[i, h * HALF : (h + 1) * HALF, :] = partial(order4[i], 1 - core, h).astype(BF16)
        ps[i, BLOCK : BLOCK + 16, :] = tail
        send(ps.at[i], pr.at[i], s4a.at[i], v4a.at[i], sib)

    def add_in(i, buf):
        pf[i, 0:BLOCK, :] += buf[0:BLOCK, :].astype(F32)
        last = buf[BLOCK : BLOCK + 16, :].astype(F32)
        pf[i, BLOCK : BLOCK + 8, :] += last[0:1, :] + last[1:2, :]

    for i in range(4):
        for h in range(2):
            pf[i, h * HALF : (h + 1) * HALF, :] = partial(order4[i], core, h)
        pf[i, BLOCK : BLOCK + 8, :] = jnp.broadcast_to(router, (8, HID))
        remote(ps.at[i], pr.at[i], s4a.at[i], v4a.at[i], l).wait_recv()
        add_in(i, pr.at[i])
        if i == 2:

            @pl.when(mid)
            def _():
                remote(ys.at[0], yrel, s4b.at[0], vrel.at[0], l).wait_recv()
                add_in(2, yrel)

        if i < 3:
            ys[i, 0:BLOCK, :] = pf[i, 0:BLOCK, :].astype(BF16)
            ys[i, BLOCK : BLOCK + 16, :] = router_rows(pf[i, BLOCK : BLOCK + 1, :], 16).astype(BF16)
            direct = remote(ys.at[i], yr.at[yq], s4b.at[i], v4b.at[yq], mate(order4[i]))
            if i == 0:

                @pl.when(mid)
                def _():
                    direct.start()

                @pl.when(outer)
                def _():
                    remote(ys.at[0], yrel, s4b.at[0], vrel.at[0], mate(1 + lax.div(yq, 3))).start()

            else:
                direct.start()
            sends.append(direct)
    for s in range(4):
        absent = (yq == s) | (yq == 3 - s) if s in (0, 3) else yq == s

        @pl.when(jnp.logical_not(absent))
        def _():
            remote(ys.at[0], yr.at[s], s4b.at[0], v4b.at[s], l).wait_recv()
            add_in(3, yr.at[s])

    router_total = pf[3, BLOCK : BLOCK + 1, :]

    for m in range(16):
        msg5[m] = jnp.concatenate(
            [pf[3, m * FEAT : (m + 1) * FEAT, :] * slot_gate, router_rows(router_total, 4)], axis=0
        ).astype(BF16)

    def exchange5(d):
        m = lax.rem(mm + d, 16)
        return remote(msg5.at[m], r5.at[col], s5.at[d], v5.at[col], home(m))

    for d in FAR_FIRST:
        exchange5(d).start()

    @pl.when(jnp.logical_not(selfish))
    def _():
        exchange5(0).start()

    @pl.when(selfish)
    def _():
        r5[col] = msg5[mm]

    for d in range(1, GROUP):
        j = lax.rem(col + d, GROUP)
        remote(msg5.at[0], r5.at[j], s5.at[0], v5.at[j], l).wait_recv()

    @pl.when(jnp.logical_not(selfish))
    def _():
        remote(msg5.at[0], r5.at[col], s5.at[0], v5.at[col], l).wait_recv()

    back = [r5[c].astype(F32) for c in range(GROUP)]
    lane = lax.broadcasted_iota(jnp.int32, (8, 256), 1) // 32
    sublane = lax.broadcasted_iota(jnp.int32, (8, 256), 0)
    for p in range(4):
        token_sum = jnp.zeros((32, 256), F32)
        gate_sum = [jnp.zeros((TOPK, TOK), F32) for _ in range(2)]
        for h in range(2):
            rows = jnp.concatenate(
                [back[8 * h + c][:, 32 * p : 32 * p + 32] for c in range(8)], axis=1
            )
            hi = jnp.where(lane == sublane, rows[28:29, :], 0.0)
            lo = jnp.where(lane == sublane, rows[29:30, :], 0.0)
            left = jnp.concatenate([rows, hi, lo], axis=0).astype(BF16)
            out = dot_nn(left, select[p, h])
            token_sum = token_sum + out[0:32]
            routed = out[32:40] + out[40:48]
            for q in range(2):
                for c in range(8):
                    gate_sum[q] = gate_sum[q] + jnp.where(
                        ids[2 * p + q] == base + float(8 * h + c),
                        routed[c : c + 1, q * TOK : (q + 1) * TOK],
                        0.0,
                    )
        for q in range(2):
            msg6[2 * p + q] = jnp.concatenate(
                [token_sum[:, q * TOK : (q + 1) * TOK], gate_sum[q]], axis=0
            )

    for d in (4, 3, 5, 2, 6, 1, 7):
        j = lax.rem(n + d, NODES)
        send(msg6.at[j], r6.at[n], s6.at[d], v6.at[n], l, node=j)
    result = msg6[n]
    for d in (1, 7, 2, 6, 3, 5, 4):
        j = lax.rem(n + d, NODES)
        remote(msg6.at[0], r6.at[j], s6.at[0], v6.at[j], l).wait_recv()
        result = result + r6[j]
    token_out[...] = result[0:FEAT].astype(BF16)
    gate_out[...] = result[32:40]

    for copy in sends:
        copy.wait_send()
    for d in range(1, 16):
        exchange2(d).wait_send()
        exchange5(d).wait_send()

    @pl.when(jnp.logical_not(selfish))
    def _():
        exchange2(0).wait_send()
        exchange5(0).wait_send()

    for s in range(4):

        @pl.when(yq == s)
        def _():
            for h in range(2):
                own = piece(yq, core, h)
                for i in [*range(len(soon[s])), 2]:
                    remote(own, own, s3.at[2 * i + h], v3y.at[0], l).wait_send()

    @pl.when(mid)
    def _():
        for h in range(2):
            there = piece(order3[0], core, h)
            remote(there, there, s3.at[14 + h], v3y.at[0], l).wait_send()


def on_device(tokens, out_grad, expert_ids, gate_weights, gate_weight, up_weight, down_weight):
    vmem = pl.BlockSpec(memory_space=pltpu.VMEM)
    hbm = pl.BlockSpec(memory_space=pltpu.HBM)
    dma = pltpu.SemaphoreType.DMA
    token_t, gate_t = pl.pallas_call(
        kernel,
        out_shape=(
            jax.ShapeDtypeStruct((FEAT, TOK), BF16),
            jax.ShapeDtypeStruct((TOPK, TOK), F32),
        ),
        in_specs=[hbm] * 7,
        out_specs=(vmem, vmem),
        scratch_shapes=[
            pltpu.VMEM((FEAT, TOK), BF16),
            pltpu.VMEM((FEAT, TOK), BF16),
            pltpu.VMEM((TOPK, TOK), jnp.int32),
            pltpu.VMEM((TOPK, TOK), F32),
            pltpu.VMEM((WIDE, 2 * HID), BF16),
            pltpu.VMEM((16, 2 * HID, HALF), BF16),
            pltpu.VMEM((HID, WIDE), BF16),
            pltpu.VMEM((16, HID, HALF), BF16),
            pltpu.VMEM((NODES, 80, TOK), BF16),
            pltpu.VMEM((80, TOK), BF16),
            pltpu.VMEM((4, 2, 256, 256), BF16),
            pltpu.VMEM((GROUP, 64, TOK), BF16),
            pltpu.VMEM((GROUP, 64, TOK), BF16),
            pltpu.VMEM((2, WIDE, TOK), BF16),
            pltpu.VMEM((4, BLOCK + 16, TOK), BF16),
            pltpu.VMEM((4, BLOCK + 16, TOK), BF16),
            pltpu.VMEM((4, BLOCK + 8, TOK), F32),
            pltpu.VMEM((4, BLOCK + 16, TOK), BF16),
            pltpu.VMEM((4, BLOCK + 16, TOK), BF16),
            pltpu.VMEM((BLOCK + 16, TOK), BF16),
            pltpu.VMEM((16, 32, TOK), BF16),
            pltpu.VMEM((GROUP, 32, TOK), BF16),
            pltpu.VMEM((NODES, 40, TOK), F32),
            pltpu.VMEM((NODES, 40, TOK), F32),
            dma((7,)),
            dma((8,)), dma((8,)),
            dma((16,)), dma((16,)),
            dma((16,)), dma((8,)), dma((8,)),
            dma((4,)), dma((4,)),
            dma((4,)), dma((4,)), dma((1,)),
            dma((16,)), dma((16,)),
            dma((8,)), dma((8,)),
        ],
        compiler_params=pltpu.CompilerParams(
            collective_id=0, has_side_effects=True, vmem_limit_bytes=64 * 1024 * 1024
        ),
        cost_estimate=pl.CostEstimate(flops=600_000_000, bytes_accessed=3_000_000, transcendentals=16384),
    )(
        tokens.T, out_grad.T, expert_ids.T, gate_weights.T, gate_weight, up_weight, down_weight
    )
    return token_t.T, gate_t.T


def solution(mesh):
    placed = (
        P("node", "local"),
        P("node", "local"),
        P("node", None),
        P("node", None),
        P(("node", "local"), None, None),
        P(("node", "local"), None, None),
        P(("node", "local"), None, None),
    )
    return jax.shard_map(
        on_device,
        mesh=mesh,
        in_specs=placed,
        out_specs=(P("node", "local"), P("node", None)),
        check_vma=False,
    )
```

```python
import jax
import jax.numpy as jnp
from jax import lax
from jax.experimental import pallas as pl
from jax.experimental.pallas import tpu as pltpu
from jax.sharding import PartitionSpec as P

MESH = pl.DeviceIdType.MESH
F32 = jnp.float32
BF16 = jnp.bfloat16

NODES = 8
GROUP = 16
SHARDS = 8
FEAT = 28
BLOCK = 448
HALF = 224
WIDE = 3584
HID = 128
CAP = 16
TOK = 128
TOPK = 8
FAR_FIRST = (8, 7, 9, 6, 10, 5, 11, 4, 12, 3, 13, 2, 14, 1, 15)


def dot_nn(left, right):
    return lax.dot_general(left, right, (((1,), (0,)), ((), ())), preferred_element_type=F32)


def dot_nt(left, right):
    return lax.dot_general(left, right, (((1,), (1,)), ((), ())), preferred_element_type=F32)


def split(value):
    high = value.astype(BF16).astype(F32)
    return high, (value - high).astype(BF16).astype(F32)


def shard_of(delta, half):
    far = lax.div(delta, 4)
    q = (1 - far) * delta + far * lax.rem(8 - delta, 4)
    return 2 * (q + half * (1 - 2 * lax.rem(q, 2))) + far


def plane_of(q, core, half):
    q = q + half * (1 - 2 * lax.rem(q, 2))
    return (1 - core) * q + core * (4 + lax.rem(4 - q, 4))


def pick(index, *options):
    out = options[0]
    for i in range(1, len(options)):
        out = jnp.where(index == i, options[i], out)
    return out


def kernel(
    tok_hbm, grad_hbm, ids_hbm, gates_hbm, wg_hbm, wu_hbm, wd_hbm,
    token_out, gate_out,
    tok_ref, grad_ref, ids_ref, gates_ref,
    wgu, wgu_t, wd, wd_b, r1, msg1, select, msg2, r2, xg, ps, pr, pf, ys, yr, yrel, msg5, r5, spread, msg6, r6,
    w_sem, s1, v1, s2, v2, s3, v3y, v3s, s4a, v4a, s4b, v4b, vrel, s5, v5, s6, v6,
):
    n = lax.axis_index("node")
    l = lax.axis_index("local")
    col = lax.div(l, SHARDS)
    zz = lax.div(l, 16)
    mm = lax.rem(l, 16)
    half_me = lax.rem(col, 2)
    core = lax.rem(l, 2)
    yq = lax.rem(lax.div(l, 2), 4)
    sib = l + 1 - 2 * core
    mid = (yq == 1) | (yq == 2)
    outer = (yq == 0) | (yq == 3)
    z_near = lax.rem(zz + plane_of(yq, core, 0), 8)
    z_far = lax.rem(zz + plane_of(yq, core, 1), 8)

    def home(m):
        later = m // 8 if isinstance(m, int) else lax.div(m, 8)
        return 16 * (z_near + later * (z_far - z_near)) + m

    def gatherer(c):
        return 8 * c + shard_of(lax.rem(zz - lax.div(c, 2) + 8, 8), half_me)

    selfish = lax.rem(l, 8) == 2 * half_me

    loads = [
        pltpu.make_async_copy(tok_hbm, tok_ref, w_sem.at[0]),
        pltpu.make_async_copy(grad_hbm, grad_ref, w_sem.at[1]),
        pltpu.make_async_copy(ids_hbm, ids_ref, w_sem.at[2]),
        pltpu.make_async_copy(gates_hbm, gates_ref, w_sem.at[3]),
        pltpu.make_async_copy(wg_hbm.at[0], wgu.at[:, pl.ds(0, HID)], w_sem.at[4]),
        pltpu.make_async_copy(wu_hbm.at[0], wgu.at[:, pl.ds(HID, HID)], w_sem.at[5]),
        pltpu.make_async_copy(wd_hbm.at[0], wd, w_sem.at[6]),
    ]
    for load in loads[:4]:
        load.start()

    barrier = pltpu.get_barrier_semaphore()

    def greet(node, local):
        pl.semaphore_signal(barrier, inc=1, device_id=(node, local), device_id_type=MESH)

    for d in range(1, NODES):
        greet(lax.rem(n + d, NODES), l)
    for d in range(1, 4):
        greet(n, col * 8 + 2 * (lax.rem(yq + d, 4)) + core)
    greet(n, sib)
    for d in range(1, GROUP):
        greet(n, gatherer(lax.rem(col + d, GROUP)))
        greet(n, home(lax.rem(mm + d, 16)))

    @pl.when(jnp.logical_not(selfish))
    def _():
        greet(n, gatherer(col))
        greet(n, home(mm))

    for load in loads[4:]:
        load.start()

    for load in loads[:4]:
        load.wait()
    gates_hi, gates_lo = split(gates_ref[...])
    msg1[...] = jnp.concatenate(
        [
            tok_ref[...].astype(F32),
            grad_ref[...].astype(F32),
            ids_ref[...].astype(F32),
            gates_hi,
            gates_lo,
        ],
        axis=0,
    ).astype(BF16)
    r1[n] = msg1[...]

    pl.semaphore_wait(barrier, 7 + 3 + 1 + 30 + jnp.where(selfish, 0, 2))

    sends = []

    def remote(src, dst, send_sem, recv_sem, local, node=None):
        return pltpu.make_async_remote_copy(
            src_ref=src,
            dst_ref=dst,
            send_sem=send_sem,
            recv_sem=recv_sem,
            device_id=(n if node is None else node, local),
            device_id_type=MESH,
        )

    def send(*args, **kw):
        copy = remote(*args, **kw)
        copy.start()
        sends.append(copy)

    for d in (4, 3, 5, 2, 6, 1, 7):
        send(msg1, r1.at[n], s1.at[d], v1.at[n], l, node=lax.rem(n + d, NODES))

    select[...] = jnp.zeros(select.shape, BF16)
    eye = (
        lax.broadcasted_iota(jnp.int32, (256, 256), 0)
        == lax.broadcasted_iota(jnp.int32, (256, 256), 1)
    ).astype(F32).astype(BF16)
    loads[4].wait()
    loads[5].wait()
    for i in range(16):
        wgu_t[i] = dot_nt(eye, wgu[i * HALF : (i + 1) * HALF, :]).astype(BF16)
    loads[6].wait()
    for i in range(16):
        wd_b[i] = wd[:, i * HALF : (i + 1) * HALF]

    for d in (1, 7, 2, 6, 3, 5, 4):
        j = lax.rem(n + d, NODES)
        remote(msg1, r1.at[j], s1.at[0], v1.at[j], l).wait_recv()

    base = (n * GROUP).astype(F32)
    expert = lax.broadcasted_iota(jnp.int32, (GROUP, TOK), 0).astype(F32)
    ids = [r1[j, 56:64, :].astype(F32) for j in range(NODES)]
    matched = []
    for j in range(NODES):
        found = jnp.zeros((GROUP, TOK), F32)
        for k in range(TOPK):
            found = jnp.where(ids[j][k : k + 1, :] == expert + base, 1.0, found)
        matched.append(found)
    matched = jnp.concatenate(matched, axis=0)
    before = (
        lax.broadcasted_iota(jnp.int32, (TOK, TOK), 0)
        < lax.broadcasted_iota(jnp.int32, (TOK, TOK), 1)
    ).astype(F32).astype(BF16)
    rank = dot_nn(matched.astype(BF16), before)
    key = jnp.where(matched > 0.0, rank, -1.0)
    slot = lax.broadcasted_iota(jnp.int32, (CAP, TOK), 0).astype(F32)
    for j in range(NODES):
        p, q = j // 2, j % 2
        for c in range(GROUP):
            row = key[j * GROUP + c : j * GROUP + c + 1, :]
            hot = jnp.where(row == slot, 1.0, 0.0).astype(BF16)
            at = ((c % 8) * 2 + q) * CAP
            select[p, c // 8, at : at + CAP, q * TOK : (q + 1) * TOK] = hot

    for h in range(2):
        picked = []
        for p in range(4):
            left = jnp.concatenate([r1[2 * p, 0:64, :], r1[2 * p + 1, 0:64, :]], axis=1)
            picked.append(dot_nt(left, select[p, h]))
        for c in range(8):
            msg2[8 * h + c] = jnp.concatenate(
                [v[:, 32 * c : 32 * c + 32] for v in picked], axis=1
            ).astype(BF16)

    def exchange2(d):
        c = lax.rem(col + d, GROUP)
        return remote(msg2.at[c], r2.at[mm], s2.at[d], v2.at[mm], gatherer(c))

    for d in FAR_FIRST:
        exchange2(d).start()

    @pl.when(jnp.logical_not(selfish))
    def _():
        exchange2(0).start()

    @pl.when(selfish)
    def _():
        r2[mm] = msg2[col]

    own_rows = []
    wanted = base + col.astype(F32)
    for j in range(NODES):
        weights = r1[j, 64:72, :].astype(F32) + r1[j, 72:80, :].astype(F32)
        weight = jnp.sum(jnp.where(ids[j] == wanted, weights, 0.0), axis=0, keepdims=True)
        own_key = jnp.sum(
            jnp.where(expert == col.astype(F32), key[j * GROUP : (j + 1) * GROUP, :], 0.0),
            axis=0,
            keepdims=True,
        )
        own_rows.append(jnp.where(own_key == slot, weight, 0.0))
    own_hi, own_lo = split(jnp.concatenate(own_rows, axis=0))
    ones = jnp.ones((8, TOK), BF16)
    slot_gate = (dot_nt(ones, own_hi.astype(BF16)) + dot_nt(ones, own_lo.astype(BF16)))[0:1, :]

    def half_at(q, k, h):
        return pl.ds(pl.multiple_of((2 * lax.rem(zz + plane_of(q, k, h), 8) + h) * HALF, 16), HALF)

    def piece(q, k, h):
        return xg.at[:, half_at(q, k, h), :]

    def mate(q):
        return col * 8 + 2 * q + core

    relay_to = 3 * (yq - 1)
    soon = ((2,), (3, 0), (0, 3), (1,))
    later = (1, 2, 1, 2)

    def gathered(m):
        remote(msg2.at[0], r2.at[m], s2.at[0], v2.at[m], l).wait_recv()

    for h in range(2):
        for i in range(8):
            m = 8 * h + i

            @pl.when(jnp.logical_not(selfish & (mm == m)))
            def _():
                gathered(m)

        for part in range(2):
            for g in range(2):
                rows = jnp.concatenate(
                    [
                        r2[8 * h + 4 * g + i, part * FEAT : (part + 1) * FEAT, :].astype(F32)
                        for i in range(4)
                    ],
                    axis=0,
                ).astype(BF16)
                at = (2 * (z_near + h * (z_far - z_near)) + h) * HALF + g * 112
                xg[part, pl.ds(pl.multiple_of(at, 16), 112), :] = rows
        own = piece(yq, core, h)
        for s in range(4):

            @pl.when(yq == s)
            def _():
                for i, p in enumerate(soon[s]):
                    remote(own, own, s3.at[2 * i + h], v3y.at[2 * s + h], mate(p)).start()

        send(own, own, s3.at[6 + h], v3s.at[2 * yq + h], sib)

    for s in range(4):

        @pl.when(yq == s)
        def _():
            for h in range(2):
                own = piece(yq, core, h)
                remote(own, own, s3.at[4 + h], v3y.at[2 * s + h], mate(later[s])).start()

    acc_gu = jnp.zeros((2 * HID, HID), F32)
    acc_h = jnp.zeros((HID, HID), F32)
    order3 = [pick(yq, 1, 3, 0, 2), pick(yq, 2, 0, 3, 1), pick(yq, 3, 2, 1, 0)]

    def add_piece(acc, q, k, h):
        b = 2 * lax.rem(zz + plane_of(q, k, h), 8) + h
        rows = half_at(q, k, h)
        return acc[0] + dot_nn(wgu_t[b], xg[0, rows, :]), acc[1] + dot_nn(wd_b[b], xg[1, rows, :])

    acc = (acc_gu, acc_h)

    def from_sibling(acc, q, h):
        there = piece(q, 1 - core, h)
        remote(there, there, s3.at[0], v3s.at[2 * q + h], l).wait_recv()
        return add_piece(acc, q, 1 - core, h)

    for h in range(2):
        acc = add_piece(acc, yq, core, h)
    for i in range(3):
        q = order3[i]
        for h in range(2):
            there = piece(q, core, h)
            remote(there, there, s3.at[0], v3y.at[2 * q + h], l).wait_recv()
            if i == 0:

                @pl.when(mid)
                def _():
                    remote(there, there, s3.at[14 + h], v3y.at[2 * q + h], mate(relay_to)).start()

            send(there, there, s3.at[8 + 2 * i + h], v3s.at[2 * q + h], sib)
            acc = add_piece(acc, q, core, h)
            acc = from_sibling(acc, yq if i == 0 else order3[i - 1], h)
    for h in range(2):
        acc = from_sibling(acc, order3[2], h)
    acc_gu, acc_h = acc

    pre_gate, pre_up = acc_gu[:HID], acc_gu[HID:]
    sigmoid = 1.0 / (1.0 + jnp.exp(-pre_gate))
    activated = pre_gate * sigmoid
    router = jnp.sum(activated * pre_up * acc_h, axis=0, keepdims=True)
    up_inner = acc_h * activated
    gate_inner = acc_h * pre_up * sigmoid * (1.0 + pre_gate * (1.0 - sigmoid))
    inner = jnp.concatenate([gate_inner, up_inner], axis=0).astype(BF16)

    def router_rows(value, rows):
        hi, lo = split(value)
        index = lax.broadcasted_iota(jnp.int32, (rows, HID), 0)
        return jnp.where(index == 0, hi, jnp.where(index == 1, lo, 0.0))

    def partial(q, k, h):
        return dot_nn(wgu[half_at(q, k, h), :], inner)

    order4 = [pick(yq, 3, 2, 1, 0), pick(yq, 2, 0, 3, 1), pick(yq, 1, 3, 0, 2), yq]
    tail = router_rows(router, 16).astype(BF16)
    for i in range(4):
        for h in range(2):
            ps[i, h * HALF : (h + 1) * HALF, :] = partial(order4[i], 1 - core, h).astype(BF16)
        ps[i, BLOCK : BLOCK + 16, :] = tail
        send(ps.at[i], pr.at[i], s4a.at[i], v4a.at[i], sib)

    def add_in(i, buf):
        pf[i, 0:BLOCK, :] += buf[0:BLOCK, :].astype(F32)
        last = buf[BLOCK : BLOCK + 16, :].astype(F32)
        pf[i, BLOCK : BLOCK + 8, :] += last[0:1, :] + last[1:2, :]

    for i in range(4):
        for h in range(2):
            pf[i, h * HALF : (h + 1) * HALF, :] = partial(order4[i], core, h)
        pf[i, BLOCK : BLOCK + 8, :] = jnp.broadcast_to(router, (8, HID))
        remote(ps.at[i], pr.at[i], s4a.at[i], v4a.at[i], l).wait_recv()
        add_in(i, pr.at[i])
        if i == 2:

            @pl.when(mid)
            def _():
                remote(ys.at[0], yrel, s4b.at[0], vrel.at[0], l).wait_recv()
                add_in(2, yrel)

        if i < 3:
            ys[i, 0:BLOCK, :] = pf[i, 0:BLOCK, :].astype(BF16)
            ys[i, BLOCK : BLOCK + 16, :] = router_rows(pf[i, BLOCK : BLOCK + 1, :], 16).astype(BF16)
            direct = remote(ys.at[i], yr.at[yq], s4b.at[i], v4b.at[yq], mate(order4[i]))
            if i == 0:

                @pl.when(mid)
                def _():
                    direct.start()

                @pl.when(outer)
                def _():
                    remote(ys.at[0], yrel, s4b.at[0], vrel.at[0], mate(1 + lax.div(yq, 3))).start()

            else:
                direct.start()
            sends.append(direct)
    for s in range(4):
        absent = (yq == s) | (yq == 3 - s) if s in (0, 3) else yq == s

        @pl.when(jnp.logical_not(absent))
        def _():
            remote(ys.at[0], yr.at[s], s4b.at[0], v4b.at[s], l).wait_recv()
            add_in(3, yr.at[s])

    router_total = pf[3, BLOCK : BLOCK + 1, :]

    for m in range(16):
        msg5[m] = jnp.concatenate(
            [pf[3, m * FEAT : (m + 1) * FEAT, :] * slot_gate, router_rows(router_total, 4)], axis=0
        ).astype(BF16)

    def exchange5(d):
        m = lax.rem(mm + d, 16)
        return remote(msg5.at[m], r5.at[col], s5.at[d], v5.at[col], home(m))

    for d in FAR_FIRST:
        exchange5(d).start()

    @pl.when(jnp.logical_not(selfish))
    def _():
        exchange5(0).start()

    @pl.when(selfish)
    def _():
        r5[col] = msg5[mm]

    for d in range(1, GROUP):
        j = lax.rem(col + d, GROUP)
        remote(msg5.at[0], r5.at[j], s5.at[0], v5.at[j], l).wait_recv()

    @pl.when(jnp.logical_not(selfish))
    def _():
        remote(msg5.at[0], r5.at[col], s5.at[0], v5.at[col], l).wait_recv()

    back = [r5[c].astype(F32) for c in range(GROUP)]
    lane = lax.broadcasted_iota(jnp.int32, (8, 256), 1) // 32
    sublane = lax.broadcasted_iota(jnp.int32, (8, 256), 0)
    for p in range(4):
        for h in range(2):
            rows = jnp.concatenate(
                [back[8 * h + c][:, 32 * p : 32 * p + 32] for c in range(8)], axis=1
            )
            hi = jnp.where(lane == sublane, rows[28:29, :], 0.0)
            lo = jnp.where(lane == sublane, rows[29:30, :], 0.0)
            spread[p, h] = jnp.concatenate([rows, hi, lo], axis=0).astype(BF16)
    for dp in (2, 1, 3, 0):
        p = lax.rem(lax.div(n, 2) + dp, 4)
        named = [r1[2 * p + q, 56:64, :].astype(F32) for q in range(2)]
        token_sum = jnp.zeros((32, 256), F32)
        gate_sum = [jnp.zeros((TOPK, TOK), F32) for _ in range(2)]
        for h in range(2):
            out = dot_nn(spread[p, h], select[p, h])
            token_sum = token_sum + out[0:32]
            routed = out[32:40] + out[40:48]
            for q in range(2):
                for c in range(8):
                    gate_sum[q] = gate_sum[q] + jnp.where(
                        named[q] == base + float(8 * h + c),
                        routed[c : c + 1, q * TOK : (q + 1) * TOK],
                        0.0,
                    )
        for q in range(2):
            msg6[2 * p + q] = jnp.concatenate(
                [token_sum[:, q * TOK : (q + 1) * TOK], gate_sum[q]], axis=0
            )
        for q in range(2 if dp else 1):
            j = 2 * p + q if dp else n + 1 - 2 * lax.rem(n, 2)
            send(msg6.at[j], r6.at[n], s6.at[2 * dp + q], v6.at[n], l, node=j)
    result = msg6[n]
    for d in (1, 7, 2, 6, 3, 5, 4):
        j = lax.rem(n + d, NODES)
        remote(msg6.at[0], r6.at[j], s6.at[0], v6.at[j], l).wait_recv()
        result = result + r6[j]
    token_out[...] = result[0:FEAT].astype(BF16)
    gate_out[...] = result[32:40]

    for copy in sends:
        copy.wait_send()
    for d in range(1, 16):
        exchange2(d).wait_send()
        exchange5(d).wait_send()

    @pl.when(jnp.logical_not(selfish))
    def _():
        exchange2(0).wait_send()
        exchange5(0).wait_send()

    for s in range(4):

        @pl.when(yq == s)
        def _():
            for h in range(2):
                own = piece(yq, core, h)
                for i in [*range(len(soon[s])), 2]:
                    remote(own, own, s3.at[2 * i + h], v3y.at[0], l).wait_send()

    @pl.when(mid)
    def _():
        for h in range(2):
            there = piece(order3[0], core, h)
            remote(there, there, s3.at[14 + h], v3y.at[0], l).wait_send()


def on_device(tokens, out_grad, expert_ids, gate_weights, gate_weight, up_weight, down_weight):
    vmem = pl.BlockSpec(memory_space=pltpu.VMEM)
    hbm = pl.BlockSpec(memory_space=pltpu.HBM)
    dma = pltpu.SemaphoreType.DMA
    token_t, gate_t = pl.pallas_call(
        kernel,
        out_shape=(
            jax.ShapeDtypeStruct((FEAT, TOK), BF16),
            jax.ShapeDtypeStruct((TOPK, TOK), F32),
        ),
        in_specs=[hbm] * 7,
        out_specs=(vmem, vmem),
        scratch_shapes=[
            pltpu.VMEM((FEAT, TOK), BF16),
            pltpu.VMEM((FEAT, TOK), BF16),
            pltpu.VMEM((TOPK, TOK), jnp.int32),
            pltpu.VMEM((TOPK, TOK), F32),
            pltpu.VMEM((WIDE, 2 * HID), BF16),
            pltpu.VMEM((16, 2 * HID, HALF), BF16),
            pltpu.VMEM((HID, WIDE), BF16),
            pltpu.VMEM((16, HID, HALF), BF16),
            pltpu.VMEM((NODES, 80, TOK), BF16),
            pltpu.VMEM((80, TOK), BF16),
            pltpu.VMEM((4, 2, 256, 256), BF16),
            pltpu.VMEM((GROUP, 64, TOK), BF16),
            pltpu.VMEM((GROUP, 64, TOK), BF16),
            pltpu.VMEM((2, WIDE, TOK), BF16),
            pltpu.VMEM((4, BLOCK + 16, TOK), BF16),
            pltpu.VMEM((4, BLOCK + 16, TOK), BF16),
            pltpu.VMEM((4, BLOCK + 8, TOK), F32),
            pltpu.VMEM((4, BLOCK + 16, TOK), BF16),
            pltpu.VMEM((4, BLOCK + 16, TOK), BF16),
            pltpu.VMEM((BLOCK + 16, TOK), BF16),
            pltpu.VMEM((16, 32, TOK), BF16),
            pltpu.VMEM((GROUP, 32, TOK), BF16),
            pltpu.VMEM((4, 2, 48, 256), BF16),
            pltpu.VMEM((NODES, 40, TOK), F32),
            pltpu.VMEM((NODES, 40, TOK), F32),
            dma((7,)),
            dma((8,)), dma((8,)),
            dma((16,)), dma((16,)),
            dma((16,)), dma((8,)), dma((8,)),
            dma((4,)), dma((4,)),
            dma((4,)), dma((4,)), dma((1,)),
            dma((16,)), dma((16,)),
            dma((8,)), dma((8,)),
        ],
        compiler_params=pltpu.CompilerParams(
            collective_id=0, has_side_effects=True, vmem_limit_bytes=64 * 1024 * 1024
        ),
        cost_estimate=pl.CostEstimate(flops=600_000_000, bytes_accessed=3_000_000, transcendentals=16384),
    )(
        tokens.T, out_grad.T, expert_ids.T, gate_weights.T, gate_weight, up_weight, down_weight
    )
    return token_t.T, gate_t.T


def solution(mesh):
    placed = (
        P("node", "local"),
        P("node", "local"),
        P("node", None),
        P("node", None),
        P(("node", "local"), None, None),
        P(("node", "local"), None, None),
        P(("node", "local"), None, None),
    )
    return jax.shard_map(
        on_device,
        mesh=mesh,
        in_specs=placed,
        out_specs=(P("node", "local"), P("node", None)),
        check_vma=False,
    )
```
